32 devices in a mesh: groups: 2 (over y), ep: 8 (over z, core), fsdp: 2 (over x).
Axes of the slice: x: 2, y: 2, z: 4, core: 2. Of those that a mesh axis runs over, the one named last changes fastest.
Arguments:
- tokens: bfloat16 [1024, 3072], P(('groups', 'ep'), 'fsdp'), parts along dimension 0, may hold values from -6 to 6
- cotangent: bfloat16 [1024, 3072], P(('groups', 'ep'), 'fsdp'), parts along dimension 0, may hold values from -6 to 6
- routes: int32 [1024, 4], P(('groups', 'ep')), parts along dimension 0, may hold values from 0 to 7, all different within a row; in each aligned block of 64 rows (0 to 63, 64 to 127, ...) at most 64 rows name the same one
- route_scale: int32 [1024, 4], P(('groups', 'ep')), parts along dimension 0, may hold values from 256 to 4096
- gate_weight: bfloat16 [8, 3072, 5376], P('ep', None, 'fsdp'), may hold values from -0.109375 to 0.109375
- up_weight: bfloat16 [8, 3072, 5376], P('ep', None, 'fsdp'), may hold values from -0.109375 to 0.109375
- down_weight: bfloat16 [8, 5376, 3072], P('ep', 'fsdp'), may hold values from -0.078125 to 0.078125
Outputs:
- token_grad: bfloat16 [1024, 3072], P(('groups', 'ep'), 'fsdp'), parts along dimension 0
- route_grad: float32 [1024, 4], P(('groups', 'ep')), parts along dimension 0
The draws below stay inside these ranges and needn't reach their ends.
There are 2 independent parts, one for each index of `groups`. The reference program is written for one: setup_inputs(seed, part) draws one part's arguments, and reference() takes and returns one part's arrays. A program takes and returns all parts, laid end to end along the dimension named above; an argument that names none is the same for every part. Nothing has to cross between parts.
Inputs may be any that keep to these rules, and one draw needn't show every extreme that they name: `routes`: each row names 4 different experts; among the 64 rows of one index of ep no expert is named by more than 64 rows, and in every draw some expert is named by exactly 64 rows of some index.
All inputs are finite; a program needn't handle non-finite values.
Results may differ from the reference program's by a relative error of at most 0.0049.
Values may be sent and summed in bfloat16 or wider, within the bound.
A program may use at most 192 MiB of HBM per device.

```python
import math
import jax
import jax.numpy as jnp
import numpy as np
from jax import lax

D = 3072
FF = 5376
TOP = 4
TOK_EP = 64
EXPERTS = 8
SLOT_CAP = 64
CAPACITY = 512
TOKENS = 512


def with_ends(drawn, rng, smallest, top_value):
    longest = drawn.shape.index(max(drawn.shape))
    spots = []
    for shift in (0, 1):
        where = [jax.random.randint(jax.random.fold_in(rng, axis), (), 0, length) for axis, length in enumerate(drawn.shape)]
        where[longest] = (where[longest] + shift) % drawn.shape[longest]
        spots.append(tuple(where))
    return drawn.at[spots[0]].set(smallest).at[spots[1]].set(top_value)


def shard_levels(stream_key, dims, cuts, low, high):
    gain, own = 1.0, jax.random.fold_in(stream_key, 6)
    for position, blocks in cuts:
        steps = jnp.exp(jax.random.uniform(jax.random.fold_in(own, position), (blocks,), jnp.float32, low / len(cuts), high / len(cuts)))
        gain = gain * jnp.repeat(steps, dims[position] // blocks).reshape([-1 if axis == position else 1 for axis in range(len(dims))])
    return gain


def deal_out(stream_key, own, number, rows, count, top, limit, slope):
    order = jax.random.permutation(stream_key, count)
    packed, usual = load_shares(count, rows * top, limit, slope, True), load_shares(count, rows * top, limit, slope, False)
    places = jnp.arange(count)

    def named(tallies, turn):
        used = int((tallies > 0).sum())
        fixed = max(1, used // 4)
        moved = fixed + (places - fixed + turn * (used - fixed)) % max(1, count - fixed)
        return jnp.zeros((count,), jnp.int32).at[order[jnp.where(places < fixed, places, moved)]].set(jnp.asarray(tallies, jnp.int32))

    tallies = jnp.where(number % 4 == 0, named(packed, number // 4), named(usual, number - number // 4 - 1))
    mixed = jax.random.permutation(jax.random.fold_in(own, 3), count)
    donor, sink = mixed[0:count // 2 * 2:2], mixed[1:count // 2 * 2:2]
    room = jnp.minimum(tallies[donor] - 1, limit - tallies[sink]) // 2
    room = jnp.where((donor == order[0]) | (sink == order[0]) | (tallies[sink] == 0), 0, jnp.maximum(room, 0))
    moved = jax.random.randint(jax.random.fold_in(own, 4), (count // 2,), 0, 1 << 20) % (room + 1)
    tallies = tallies.at[donor].add(-moved).at[sink].add(moved)
    labels = jnp.searchsorted(jnp.cumsum(tallies), jnp.arange(rows * top), side="right").astype(jnp.int32)
    grid = labels.reshape(top, rows).T
    grid = grid[jax.random.permutation(jax.random.fold_in(own, 1), rows)]
    turn = jax.random.randint(jax.random.fold_in(own, 2), (rows, 1), 0, top)
    return jnp.take_along_axis(grid, (jnp.arange(top)[None, :] + turn) % top, axis=1)


def load_shares(count, total, most, slope, full):
    weights = [(1 << 20) // math.isqrt(standing ** slope) + 1 for standing in range(1, count + 1)]
    largest = most if full else min(most, max(-(-total // count), total * weights[0] // sum(weights)))
    least = 1 if total - largest >= count - 1 else 0
    given, spare = [largest] + [least] * (count - 1), total - largest - least * (count - 1)
    while spare > 0:
        movable = [i for i in range(1, count) if given[i] < largest] or [i for i in range(1, count) if given[i] < most]
        pool, remaining = sum([weights[i] for i in movable]), spare
        for i in movable:
            more = min(most - given[i], max(1, remaining * weights[i] // pool), spare)
            given[i] = given[i] + more
            spare = spare - more
    return np.array(given)


def gaussian(stream_key, dims, spread, most, cuts=(), kind=jnp.bfloat16):
    loudness = shard_levels(stream_key, dims, cuts, -0.22, 0.18) if cuts else 1.0
    drawn = jax.random.normal(stream_key, dims, jnp.float32) * spread * loudness
    return jnp.minimum(jnp.maximum(drawn, -most), most).astype(kind)


def setup_inputs(seed: int = 0, part: int = 0) -> dict:
    splits = jax.random.split(jax.random.key(seed), 8)
    own_keys = jax.random.split(jax.random.fold_in(splits[7], part), 8)
    tokens = gaussian(own_keys[0], (TOKENS, D), 1.0, 6.0, ((0, 8), (1, 2)))
    cotangent = gaussian(own_keys[1], (TOKENS, D), 1.0, 6.0, ((0, 8), (1, 2)))
    routes_keys = jax.random.split(jax.random.fold_in(own_keys[2], 1), TOKENS // TOK_EP)
    routes_turns = jax.random.permutation(jax.random.fold_in(own_keys[2], 3), TOKENS // TOK_EP)
    routes = jax.vmap(lambda own, number: deal_out(jax.random.fold_in(own_keys[2], 2), own, number, TOK_EP, EXPERTS, TOP, SLOT_CAP, 2))(routes_keys, routes_turns).reshape((TOKENS, TOP))
    route_scale = with_ends(jax.random.randint(own_keys[3], (TOKENS, TOP), 256, 4097), jax.random.fold_in(own_keys[3], 1), 256, 4096).astype(jnp.int32)
    gate_weight = gaussian(splits[4], (EXPERTS, D, FF), D ** -0.5, 0.109375, ((0, 8), (2, 2)))
    up_weight = gaussian(splits[5], (EXPERTS, D, FF), D ** -0.5, 0.109375, ((0, 8), (2, 2)))
    down_weight = gaussian(splits[6], (EXPERTS, FF, D), FF ** -0.5, 0.078125, ((0, 8), (1, 2)))
    return {"tokens": tokens, "cotangent": cotangent, "routes": routes, "route_scale": route_scale, "gate_weight": gate_weight, "up_weight": up_weight, "down_weight": down_weight}


def contract_last(left, right):
    return lax.dot_general(left, right, (((1,), (1,)), ((), ())), preferred_element_type=jnp.float32)

def reference(tokens, cotangent, routes, route_scale, gate_weight, up_weight, down_weight):
    total = tokens.shape[0]
    blocks = (jnp.arange(total) // TOK_EP).astype(jnp.int32)
    weights = route_scale.astype(jnp.float32) / 4096.0
    positions = jnp.arange(total, dtype=jnp.int32)
    inverse = 1.0 / math.sqrt(FF)

    def per_expert(carry, expert):
        grad_sum, route_sum = carry
        matched = routes == expert
        chosen = jnp.any(matched, axis=1)
        picked = chosen.astype(jnp.int32).reshape(-1, TOK_EP)
        ranking = (jnp.cumsum(picked, axis=1) - picked).reshape(-1)
        slot_index = jnp.where(chosen, blocks * SLOT_CAP + ranking, CAPACITY).astype(jnp.int32)
        source = jnp.zeros((CAPACITY,), jnp.int32).at[slot_index].set(positions, mode='drop')
        token_weight = lax.optimization_barrier(jnp.sum(jnp.where(matched, weights, 0.0), axis=1))
        slot_weight = jnp.zeros((CAPACITY,), jnp.float32).at[slot_index].set(token_weight, mode='drop')
        gate_here = lax.dynamic_index_in_dim(gate_weight, expert, 0, keepdims=False)
        up_here = lax.dynamic_index_in_dim(up_weight, expert, 0, keepdims=False)
        down_here = lax.dynamic_index_in_dim(down_weight, expert, 0, keepdims=False)
        tile_tok = tokens[source]
        tile_cot = cotangent[source]
        gate_proj = jnp.dot(tile_tok, gate_here, preferred_element_type=jnp.float32)
        upward = jnp.dot(tile_tok, up_here, preferred_element_type=jnp.float32)
        backward = contract_last(tile_cot, down_here)
        sigmoid_gate = jax.nn.sigmoid(gate_proj)
        activated = gate_proj * sigmoid_gate
        route_tile = lax.optimization_barrier(jnp.sum(activated * upward * backward, axis=1)) * inverse
        scaled = slot_weight[:, None] * backward
        up_grad = (scaled * activated).astype(jnp.bfloat16)
        gate_grad = (scaled * upward * sigmoid_gate * (1.0 + gate_proj * (1.0 - sigmoid_gate))).astype(jnp.bfloat16)
        partial_value = contract_last(gate_grad, gate_here) + contract_last(up_grad, up_here)
        clipped = jnp.minimum(slot_index, CAPACITY - 1)
        grad_sum = grad_sum + jnp.where(chosen[:, None], partial_value[clipped], 0.0)
        route_sum = route_sum + jnp.where(matched, route_tile[clipped][:, None], 0.0)
        return ((grad_sum, route_sum), None)
    start = (jnp.zeros((total, D), jnp.float32), jnp.zeros((total, TOP), jnp.float32))
    (grad_sum, route_sum), unused = lax.scan(per_expert, start, jnp.arange(EXPERTS, dtype=jnp.int32))
    return (grad_sum.astype(jnp.bfloat16), route_sum)
```

```python
import functools
import math

import jax
import jax.numpy as jnp
from jax import lax
from jax.experimental import pallas as pl
from jax.experimental.pallas import tpu as pltpu
from jax.sharding import PartitionSpec as P

FF = 5376
MESH = pl.DeviceIdType.MESH
LANES = 128
TILE = 512


def contract_last(left, right):
    return lax.dot_general(
        left, right, (((1,), (1,)), ((), ())), preferred_element_type=jnp.float32
    )


def kernel(
    nz, nx, widths, tok_ref, cot_ref, routes_ref, scale_ref, wg_hbm, wu_hbm, wd_hbm,
    out_ref, rg_ref,
    X, Wg, Wu, Wd, acc, rp, wv, WS, WR, RS, RR, SC, RC, SX, RX, S2, SZ, RZ,
    wsem, zs, zr, xs, xr, cs, cr, bs, br, ps, pr, ccs, ccr, cxs, cxr, czs, czr,
):
    ep = 2 * nz
    n = ep * nx
    nt = len(widths)
    dx = tok_ref.shape[1]
    hr = tok_ref.shape[0] // 2
    mine = nz * hr
    g = lax.axis_index("groups")
    e = lax.axis_index("ep")
    x = lax.axis_index("fsdp")
    z, c = lax.div(e, 2), lax.rem(e, 2)
    me = e * nx + x

    def rows(cc, zz, count=1):
        return pl.ds(pl.multiple_of((cc * nz + zz) * hr, hr), hr * count)

    def cols(xx):
        return pl.ds(pl.multiple_of(xx * dx, LANES), dx)

    def remote(src, dst, ss, rs, dev):
        return pltpu.make_async_remote_copy(
            src_ref=src, dst_ref=dst, send_sem=ss, recv_sem=rs,
            device_id=dev, device_id_type=MESH,
        )

    def tile_copies(t, slot):
        w, off = widths[t], sum(widths[:t])
        return (
            pltpu.make_async_copy(wg_hbm.at[0, :, pl.ds(off, w)], Wg.at[slot, :, pl.ds(0, w)], wsem.at[slot, 0]),
            pltpu.make_async_copy(wu_hbm.at[0, :, pl.ds(off, w)], Wu.at[slot, :, pl.ds(0, w)], wsem.at[slot, 1]),
            pltpu.make_async_copy(wd_hbm.at[0, pl.ds(off, w), :], Wd.at[slot, pl.ds(0, w), :], wsem.at[slot, 2]),
        )

    def main_copies(t, slot):
        w = widths[0]
        off = pl.multiple_of(t * w, w)
        return (
            pltpu.make_async_copy(wg_hbm.at[0, :, pl.ds(off, w)], Wg.at[slot, :, pl.ds(0, w)], wsem.at[slot, 0]),
            pltpu.make_async_copy(wu_hbm.at[0, :, pl.ds(off, w)], Wu.at[slot, :, pl.ds(0, w)], wsem.at[slot, 1]),
            pltpu.make_async_copy(wd_hbm.at[0, pl.ds(off, w), :], Wd.at[slot, pl.ds(0, w), :], wsem.at[slot, 2]),
        )

    for copy in tile_copies(0, 0):
        copy.start()

    for h in range(2):
        X[h, 0, rows(c, z), cols(x)] = tok_ref[h * hr:(h + 1) * hr, :]
        X[h, 1, rows(c, z), cols(x)] = cot_ref[h * hr:(h + 1) * hr, :]
    full = 2 * hr
    lane = lax.broadcasted_iota(jnp.int32, (full, LANES), 1)
    sub = lax.broadcasted_iota(jnp.int32, (full, LANES), 0)
    weights = scale_ref[...].astype(jnp.float32) / 4096.0
    routes = routes_ref[...]

    for expert in range(ep):
        column = jnp.sum(jnp.where(routes == expert, weights, 0.0), axis=1, keepdims=True)
        row = jnp.sum(jnp.where(lane == sub, column, 0.0), axis=0, keepdims=True)
        WS[expert] = jnp.broadcast_to(row, (8, LANES))

    barrier = pltpu.get_barrier_semaphore()

    def greet(d, carry):
        other = lax.rem(me + d, n)
        pl.semaphore_signal(
            barrier, inc=1, device_id=(g, lax.div(other, nx), lax.rem(other, nx)), device_id_type=MESH
        )
        return carry

    lax.fori_loop(1, n, greet, 0)
    acc[...] = jnp.zeros_like(acc)
    rp[...] = jnp.zeros_like(rp)
    pl.semaphore_wait(barrier, n - 1)

    def zcopy(h, zb, way):
        part = X.at[h, :, rows(c, zb), cols(x)]
        to = z + 1 if way == 0 else z - 1
        return remote(part, part, zs.at[h, zb, way], zr.at[h, zb], (g, 2 * to + c, x))

    def xcopy(h, zb, d):
        part = X.at[h, :, rows(c, zb), cols(x)]
        return remote(part, part, xs.at[h, d, zb], xr.at[h, d, zb], (g, e, lax.rem(x + d, nx)))

    def xarrival(h, zb, d):
        part = X.at[h, :, rows(c, zb), cols(lax.rem(x - d + nx, nx))]
        return remote(part, part, xs.at[h, d, zb], xr.at[h, d, zb], (g, e, lax.rem(x + d, nx)))

    def ccopy(h, zb, xb):
        part = X.at[h, :, rows(c, zb), cols(xb)]
        return remote(part, part, cs.at[h, xb, zb], cr.at[h, xb, zb], (g, 2 * z + 1 - c, x))

    def carrival(h, zb, xb):
        part = X.at[h, :, rows(1 - c, zb), cols(xb)]
        return remote(part, part, cs.at[h, xb, zb], cr.at[h, xb, zb], (g, 2 * z + 1 - c, x))

    def spread(h, zb):
        for d in range(1, nx):
            xcopy(h, zb, d).start()
        ccopy(h, zb, x).start()

    def own(h):
        @pl.when(z < nz - 1)
        def _():
            zcopy(h, z, 0).start()

        @pl.when(z > 0)
        def _():
            zcopy(h, z, 1).start()

        spread(h, z)

    def step(h, s):
        @pl.when(z - s >= 0)
        def _():
            zcopy(h, z - s, 0).wait_recv()

            @pl.when(z < nz - 1)
            def _():
                zcopy(h, z - s, 0).start()

            spread(h, z - s)

        @pl.when(z + s < nz)
        def _():
            zcopy(h, z + s, 1).wait_recv()

            @pl.when(z > 0)
            def _():
                zcopy(h, z + s, 1).start()

            spread(h, z + s)

    def at_distance(s, fn):
        if s == 0:
            fn(z)
            return

        @pl.when(z - s >= 0)
        def _():
            fn(z - s)

        @pl.when(z + s < nz)
        def _():
            fn(z + s)

    def xwait(h, s):
        def one(zb):
            for d in range(1, nx):
                xarrival(h, zb, d).wait_recv()
                ccopy(h, zb, lax.rem(x - d + nx, nx)).start()

        at_distance(s, one)

    def cwait(h):
        for zb in range(nz):
            for xb in range(nx):
                carrival(h, zb, xb).wait_recv()

    def drain_gather(h):
        for zb in range(nz):
            @pl.when(jnp.logical_and(zb <= z, z < nz - 1))
            def _():
                zcopy(h, zb, 0).wait_send()

            @pl.when(jnp.logical_and(zb >= z, z > 0))
            def _():
                zcopy(h, zb, 1).wait_send()

            for d in range(1, nx):
                xcopy(h, zb, d).wait_send()
            for xb in range(nx):
                ccopy(h, zb, xb).wait_send()

    def bcopy(d):
        to = lax.rem(e + d, ep)
        return remote(WS.at[to], WR.at[e], bs.at[to], br.at[e], (g, to, x))

    def barrival(d):
        frm = lax.rem(e - d + ep, ep)
        return remote(WS.at[frm], WR.at[frm], bs.at[frm], br.at[frm], (g, frm, x))

    own(0)
    lax.fori_loop(1, ep, lambda d, carry: (bcopy(d).start(), carry)[1], 0)
    for s in range(1, nz):
        step(0, s)
        xwait(0, s - 1)
    own(1)
    xwait(0, nz - 1)
    lax.fori_loop(1, ep, lambda d, carry: (barrival(d).wait_recv(), carry)[1], 0)
    WR[e] = WS[e]
    hlane = lax.broadcasted_iota(jnp.int32, (hr, LANES), 1)
    hsub = lax.broadcasted_iota(jnp.int32, (hr, LANES), 0)
    for cc in range(2):
        for zz in range(nz):
            row = WR[2 * zz + cc][0:1, :]
            for h in range(2):
                column = jnp.sum(jnp.where(hlane == hsub + h * hr, row, 0.0), axis=1, keepdims=True)
                q = (cc * nz + zz) * hr
                wv[h, q:q + hr, :] = jnp.broadcast_to(column, (hr, LANES))
    cwait(0)

    def core_copy(h):
        return remote(SC.at[h], RC.at[h], ccs.at[h], ccr.at[h], (g, 2 * z + 1 - c, x))

    def cx_copy(h, d):
        return remote(SX.at[h, d - 1], RX.at[h, d - 1], cxs.at[h, d], cxr.at[h, d], (g, e, lax.rem(x + d, nx)))

    def cz_copy(h, d):
        to = lax.rem(z + d, nz)
        part = SZ.at[h, pl.ds(pl.multiple_of(to * hr, hr), hr), :]
        return remote(part, RZ.at[h, d - 1], czs.at[h, d], czr.at[h, d], (g, 2 * to + c, x))

    def stage_core(h):
        SC[h] = acc[h, rows(1 - c, 0, nz), :].astype(jnp.bfloat16)
        core_copy(h).start()

    def stage_x(h):
        core_copy(h).wait_recv()
        for d in range(1, nx):
            there = cols(lax.rem(x + d, nx))
            SX[h, d - 1] = (
                acc[h, rows(c, 0, nz), there] + RC[h, :, there].astype(jnp.float32)
            ).astype(jnp.bfloat16)
            cx_copy(h, d).start()
        S2[h] = acc[h, rows(c, 0, nz), cols(x)] + RC[h, :, cols(x)].astype(jnp.float32)

    def stage_z(h):
        total = S2[h]
        for d in range(1, nx):
            cx_copy(h, d).wait_recv()
            total = total + RX[h, d - 1].astype(jnp.float32)
        S2[h] = total
        SZ[h] = total.astype(jnp.bfloat16)
        for d in range(1, nz):
            cz_copy(h, d).start()

    def stage_out(h):
        total = S2[h, pl.ds(pl.multiple_of(z * hr, hr), hr), :]
        for d in range(1, nz):
            cz_copy(h, d).wait_recv()
            total = total + RZ[h, d - 1].astype(jnp.float32)
        out_ref[h * hr:(h + 1) * hr, :] = total.astype(jnp.bfloat16)

    def compute(h, slot, w):
        gate = jnp.dot(X[h, 0], Wg[slot, :, 0:w], preferred_element_type=jnp.float32)
        up = jnp.dot(X[h, 0], Wu[slot, :, 0:w], preferred_element_type=jnp.float32)
        back = contract_last(X[h, 1], Wd[slot, 0:w, :])
        sig = jax.nn.sigmoid(gate)
        act = gate * sig
        rp[h] += jnp.sum(act * up * back, axis=1, keepdims=True)
        scaled = wv[h][:, 0:1] * back
        up_grad = (scaled * act).astype(jnp.bfloat16)
        gate_grad = (scaled * up * sig * (1.0 + gate * (1.0 - sig))).astype(jnp.bfloat16)
        depth = acc.shape[2]
        chunk = 512 if depth % 512 == 0 else LANES

        def part(j, carry):
            at = pl.ds(pl.multiple_of(j * chunk, chunk), chunk)
            acc[h, :, at] += contract_last(gate_grad, Wg[slot, at, 0:w]) + contract_last(
                up_grad, Wu[slot, at, 0:w]
            )
            return carry

        lax.fori_loop(0, depth // chunk, part, 0)

    events = {}

    def plan(i, fn):
        events.setdefault(i, []).append(fn)

    for s in range(1, nz + 1):
        def event(s=s):
            if s < nz:
                step(1, s)
            xwait(1, s - 1)

        plan(min(s, nt - 1), event)
    plan(nt, lambda: cwait(1))
    plan(nt, lambda: stage_core(0))
    plan(min(nt + 1, 2 * nt - 1), lambda: stage_x(0))
    plan(min(nt + 3, 2 * nt - 1), lambda: stage_z(0))

    def iteration(i, carry):
        h = lax.div(i, nt)
        t = lax.rem(i, nt)
        slot = lax.rem(i, 2) if nt > 1 else 0
        for at in sorted(events):
            @pl.when(i == at)
            def _():
                for fn in events[at]:
                    fn()

        if nt == 1:
            @pl.when(i == 0)
            def _():
                for copy in tile_copies(0, 0):
                    copy.wait()

            compute(h, 0, widths[0])
            return carry

        following = lax.rem(t + 1, nt)
        other = 1 - slot

        @pl.when(jnp.logical_and(i + 1 < 2 * nt, following < nt - 1))
        def _():
            for copy in main_copies(following, other):
                copy.start()

        @pl.when(jnp.logical_and(i + 1 < 2 * nt, following == nt - 1))
        def _():
            for copy in tile_copies(nt - 1, other):
                copy.start()

        @pl.when(t < nt - 1)
        def _():
            for copy in main_copies(t, slot):
                copy.wait()
            compute(h, slot, widths[0])

        @pl.when(t == nt - 1)
        def _():
            for copy in tile_copies(nt - 1, slot):
                copy.wait()
            compute(h, slot, widths[nt - 1])

        return carry

    lax.fori_loop(0, 2 * nt, iteration, 0)

    stage_core(1)
    for cc in range(2):
        for zz in range(nz):
            q = (cc * nz + zz) * hr
            row = jnp.zeros((1, LANES), jnp.float32)
            for h in range(2):
                row = row + jnp.sum(
                    jnp.where(hlane == hsub + h * hr, rp[h, q:q + hr, :], 0.0), axis=0, keepdims=True
                )
            RS[2 * zz + cc] = jnp.broadcast_to(row, (8, LANES))

    def pcopy(d):
        other = lax.rem(me + d, n)
        oe, ox = lax.div(other, nx), lax.rem(other, nx)
        return remote(RS.at[oe], RR.at[me], ps.at[other], pr.at[me], (g, oe, ox))

    def parrival(d):
        frm = lax.rem(me - d + n, n)
        fe, fx = lax.div(frm, nx), lax.rem(frm, nx)
        return remote(RS.at[fe], RR.at[frm], ps.at[frm], pr.at[frm], (g, fe, fx))

    lax.fori_loop(1, n, lambda d, carry: (pcopy(d).start(), carry)[1], 0)
    stage_x(1)
    stage_out(0)
    stage_z(1)
    lax.fori_loop(1, n, lambda d, carry: (parrival(d).wait_recv(), carry)[1], 0)
    RR[me] = RS[e]
    grad = jnp.zeros(routes.shape, jnp.float32)
    for expert in range(ep):
        row = jnp.zeros((1, LANES), jnp.float32)
        for xx in range(nx):
            row = row + RR[expert * nx + xx][0:1, :]
        column = jnp.sum(jnp.where(lane == sub, row, 0.0), axis=1, keepdims=True)
        grad = grad + jnp.where(routes == expert, column, 0.0)
    rg_ref[...] = grad * (1.0 / math.sqrt(FF))
    stage_out(1)

    for h in range(2):
        drain_gather(h)
        core_copy(h).wait_send()
        for d in range(1, nx):
            cx_copy(h, d).wait_send()
        for d in range(1, nz):
            cz_copy(h, d).wait_send()
    lax.fori_loop(1, ep, lambda d, carry: (bcopy(d).wait_send(), carry)[1], 0)
    lax.fori_loop(1, n, lambda d, carry: (pcopy(d).wait_send(), carry)[1], 0)


def shards(tokens, cotangent, routes, route_scale, gate_weight, up_weight, down_weight):
    ep, nx = lax.axis_size("ep"), lax.axis_size("fsdp")
    nz = ep // 2
    n = ep * nx
    block, dx = tokens.shape
    hr = block // 2
    depth, hidden = gate_weight.shape[1:]
    half = ep * hr
    mine = nz * hr
    if hidden % LANES == 0 and hidden > TILE:
        widths = [TILE] * (hidden // TILE) + ([hidden % TILE] if hidden % TILE else [])
    else:
        widths = [hidden]
    slots = min(2, len(widths))
    bf16, f32 = jnp.bfloat16, jnp.float32
    dma = pltpu.SemaphoreType.DMA
    vmem = pl.BlockSpec(memory_space=pltpu.VMEM)
    return pl.pallas_call(
        functools.partial(kernel, nz, nx, widths),
        out_shape=(
            jax.ShapeDtypeStruct((block, dx), bf16),
            jax.ShapeDtypeStruct(routes.shape, f32),
        ),
        in_specs=[vmem] * 4 + [pl.BlockSpec(memory_space=pl.ANY)] * 3,
        out_specs=(vmem, vmem),
        scratch_shapes=[
            pltpu.VMEM((2, 2, half, depth), bf16),
            pltpu.VMEM((slots, depth, widths[0]), bf16),
            pltpu.VMEM((slots, depth, widths[0]), bf16),
            pltpu.VMEM((slots, widths[0], depth), bf16),
            pltpu.VMEM((2, half, depth), f32),
            pltpu.VMEM((2, half, LANES), f32),
            pltpu.VMEM((2, half, LANES), f32),
            pltpu.VMEM((ep, 8, LANES), f32),
            pltpu.VMEM((ep, 8, LANES), f32),
            pltpu.VMEM((ep, 8, LANES), f32),
            pltpu.VMEM((n, 8, LANES), f32),
            pltpu.VMEM((2, mine, depth), bf16),
            pltpu.VMEM((2, mine, depth), bf16),
            pltpu.VMEM((2, nx - 1, mine, dx), bf16),
            pltpu.VMEM((2, nx - 1, mine, dx), bf16),
            pltpu.VMEM((2, mine, dx), f32),
            pltpu.VMEM((2, mine, dx), bf16),
            pltpu.VMEM((2, nz - 1, hr, dx), bf16),
            dma((slots, 3)),
            dma((2, nz, 2)),
            dma((2, nz)),
            dma((2, nx, nz)),
            dma((2, nx, nz)),
            dma((2, nx, nz)),
            dma((2, nx, nz)),
            dma((ep,)),
            dma((ep,)),
            dma((n,)),
            dma((n,)),
            dma((2,)),
            dma((2,)),
            dma((2, nx)),
            dma((2, nx)),
            dma((2, nz)),
            dma((2, nz)),
        ],
        compiler_params=pltpu.CompilerParams(
            collective_id=0, has_side_effects=True, vmem_limit_bytes=62 * 1024 * 1024
        ),
        cost_estimate=pl.CostEstimate(
            flops=20 * half * depth * hidden, bytes_accessed=12 * depth * hidden, transcendentals=0
        ),
    )(tokens, cotangent, routes, route_scale, gate_weight, up_weight, down_weight)


def solution(mesh):
    in_specs = (
        P(("groups", "ep"), "fsdp"),
        P(("groups", "ep"), "fsdp"),
        P(("groups", "ep"), None),
        P(("groups", "ep"), None),
        P("ep", None, "fsdp"),
        P("ep", None, "fsdp"),
        P("ep", "fsdp", None),
    )
    out_specs = (P(("groups", "ep"), "fsdp"), P(("groups", "ep"), None))
    return jax.shard_map(shards, mesh=mesh, in_specs=in_specs, out_specs=out_specs, check_vma=False)
```

```python
import functools
import math

import jax
import jax.numpy as jnp
from jax import lax
from jax.experimental import pallas as pl
from jax.experimental.pallas import tpu as pltpu
from jax.sharding import PartitionSpec as P

FF = 5376
MESH = pl.DeviceIdType.MESH
LANES = 128
TILE = 512


def contract_last(left, right):
    return lax.dot_general(
        left, right, (((1,), (1,)), ((), ())), preferred_element_type=jnp.float32
    )


def kernel(
    nz, nx, widths, tok_ref, cot_ref, routes_ref, scale_ref, wg_hbm, wu_hbm, wd_hbm,
    out_ref, rg_ref,
    X, Wg, Wu, Wd, Vg, Vu, GG, UG, acc, rp, wv, WS, WR, RS, RR, SC, RC, SX, RX, S2, SZ, RZ,
    wsem, vsem, zs, zr, xs, xr, cs, cr, bs, br, ps, pr, ccs, ccr, cxs, cxr, czs, czr,
):
    ep = 2 * nz
    n = ep * nx
    nt = len(widths)
    dx = tok_ref.shape[1]
    hr = tok_ref.shape[0] // 2
    mine = nz * hr
    half = 2 * mine
    cw = acc.shape[2]
    kc = dx // cw
    steps = kc * nx
    g = lax.axis_index("groups")
    e = lax.axis_index("ep")
    x = lax.axis_index("fsdp")
    z, c = lax.div(e, 2), lax.rem(e, 2)
    me = e * nx + x

    def rows(cc, zz, count=1):
        return pl.ds(pl.multiple_of((cc * nz + zz) * hr, hr), hr * count)

    def cols(xx):
        return pl.ds(pl.multiple_of(xx * dx, LANES), dx)

    def remote(src, dst, ss, rs, dev):
        return pltpu.make_async_remote_copy(
            src_ref=src, dst_ref=dst, send_sem=ss, recv_sem=rs,
            device_id=dev, device_id_type=MESH,
        )

    def tile_copies(t, slot):
        w, off = widths[t], sum(widths[:t])
        return (
            pltpu.make_async_copy(wg_hbm.at[0, :, pl.ds(off, w)], Wg.at[slot, :, pl.ds(0, w)], wsem.at[slot, 0]),
            pltpu.make_async_copy(wu_hbm.at[0, :, pl.ds(off, w)], Wu.at[slot, :, pl.ds(0, w)], wsem.at[slot, 1]),
            pltpu.make_async_copy(wd_hbm.at[0, pl.ds(off, w), :], Wd.at[slot, pl.ds(0, w), :], wsem.at[slot, 2]),
        )

    def main_copies(t, slot):
        w = widths[0]
        off = pl.multiple_of(t * w, w)
        return (
            pltpu.make_async_copy(wg_hbm.at[0, :, pl.ds(off, w)], Wg.at[slot, :, pl.ds(0, w)], wsem.at[slot, 0]),
            pltpu.make_async_copy(wu_hbm.at[0, :, pl.ds(off, w)], Wu.at[slot, :, pl.ds(0, w)], wsem.at[slot, 1]),
            pltpu.make_async_copy(wd_hbm.at[0, pl.ds(off, w), :], Wd.at[slot, pl.ds(0, w), :], wsem.at[slot, 2]),
        )

    for copy in tile_copies(0, 0):
        copy.start()

    for h in range(2):
        X[h, 0, rows(c, z), cols(x)] = tok_ref[h * hr:(h + 1) * hr, :]
        X[h, 1, rows(c, z), cols(x)] = cot_ref[h * hr:(h + 1) * hr, :]
    full = 2 * hr
    lane = lax.broadcasted_iota(jnp.int32, (full, LANES), 1)
    sub = lax.broadcasted_iota(jnp.int32, (full, LANES), 0)
    weights = scale_ref[...].astype(jnp.float32) / 4096.0
    routes = routes_ref[...]

    for expert in range(ep):
        column = jnp.sum(jnp.where(routes == expert, weights, 0.0), axis=1, keepdims=True)
        row = jnp.sum(jnp.where(lane == sub, column, 0.0), axis=0, keepdims=True)
        WS[expert] = jnp.broadcast_to(row, (8, LANES))

    barrier = pltpu.get_barrier_semaphore()

    def greet(d, carry):
        other = lax.rem(me + d, n)
        pl.semaphore_signal(
            barrier, inc=1, device_id=(g, lax.div(other, nx), lax.rem(other, nx)), device_id_type=MESH
        )
        return carry

    lax.fori_loop(1, n, greet, 0)
    rp[...] = jnp.zeros_like(rp)
    pl.semaphore_wait(barrier, n - 1)

    def zcopy(h, zb, way):
        part = X.at[h, :, rows(c, zb), cols(x)]
        to = z + 1 if way == 0 else z - 1
        return remote(part, part, zs.at[h, zb, way], zr.at[h, zb], (g, 2 * to + c, x))

    def xcopy(h, zb, d):
        part = X.at[h, :, rows(c, zb), cols(x)]
        return remote(part, part, xs.at[h, d, zb], xr.at[h, d, zb], (g, e, lax.rem(x + d, nx)))

    def xarrival(h, zb, d):
        part = X.at[h, :, rows(c, zb), cols(lax.rem(x - d + nx, nx))]
        return remote(part, part, xs.at[h, d, zb], xr.at[h, d, zb], (g, e, lax.rem(x + d, nx)))

    def ccopy(h, zb, xb):
        part = X.at[h, :, rows(c, zb), cols(xb)]
        return remote(part, part, cs.at[h, xb, zb], cr.at[h, xb, zb], (g, 2 * z + 1 - c, x))

    def carrival(h, zb, xb):
        part = X.at[h, :, rows(1 - c, zb), cols(xb)]
        return remote(part, part, cs.at[h, xb, zb], cr.at[h, xb, zb], (g, 2 * z + 1 - c, x))

    def spread(h, zb):
        for d in range(1, nx):
            xcopy(h, zb, d).start()
        ccopy(h, zb, x).start()

    def own(h):
        @pl.when(z < nz - 1)
        def _():
            zcopy(h, z, 0).start()

        @pl.when(z > 0)
        def _():
            zcopy(h, z, 1).start()

        spread(h, z)

    def step(h, s):
        @pl.when(z - s >= 0)
        def _():
            zcopy(h, z - s, 0).wait_recv()

            @pl.when(z < nz - 1)
            def _():
                zcopy(h, z - s, 0).start()

            spread(h, z - s)

        @pl.when(z + s < nz)
        def _():
            zcopy(h, z + s, 1).wait_recv()

            @pl.when(z > 0)
            def _():
                zcopy(h, z + s, 1).start()

            spread(h, z + s)

    def at_distance(s, fn):
        if s == 0:
            fn(z)
            return

        @pl.when(z - s >= 0)
        def _():
            fn(z - s)

        @pl.when(z + s < nz)
        def _():
            fn(z + s)

    def xwait(h, s):
        def one(zb):
            for d in range(1, nx):
                xarrival(h, zb, d).wait_recv()
                ccopy(h, zb, lax.rem(x - d + nx, nx)).start()

        at_distance(s, one)

    def cwait(h):
        for zb in range(nz):
            for xb in range(nx):
                carrival(h, zb, xb).wait_recv()

    def drain_gather(h):
        for zb in range(nz):
            @pl.when(jnp.logical_and(zb <= z, z < nz - 1))
            def _():
                zcopy(h, zb, 0).wait_send()

            @pl.when(jnp.logical_and(zb >= z, z > 0))
            def _():
                zcopy(h, zb, 1).wait_send()

            for d in range(1, nx):
                xcopy(h, zb, d).wait_send()
            for xb in range(nx):
                ccopy(h, zb, xb).wait_send()

    def bcopy(d):
        to = lax.rem(e + d, ep)
        return remote(WS.at[to], WR.at[e], bs.at[to], br.at[e], (g, to, x))

    def barrival(d):
        frm = lax.rem(e - d + ep, ep)
        return remote(WS.at[frm], WR.at[frm], bs.at[frm], br.at[frm], (g, frm, x))

    own(0)
    lax.fori_loop(1, ep, lambda d, carry: (bcopy(d).start(), carry)[1], 0)
    for s in range(1, nz):
        step(0, s)
        xwait(0, s - 1)
    own(1)
    xwait(0, nz - 1)
    lax.fori_loop(1, ep, lambda d, carry: (barrival(d).wait_recv(), carry)[1], 0)
    WR[e] = WS[e]
    hlane = lax.broadcasted_iota(jnp.int32, (hr, LANES), 1)
    hsub = lax.broadcasted_iota(jnp.int32, (hr, LANES), 0)
    for cc in range(2):
        for zz in range(nz):
            row = WR[2 * zz + cc][0:1, :]
            for h in range(2):
                column = jnp.sum(jnp.where(hlane == hsub + h * hr, row, 0.0), axis=1, keepdims=True)
                q = (cc * nz + zz) * hr
                wv[h, q:q + hr, :] = jnp.broadcast_to(column, (hr, LANES))
    cwait(0)

    def chunk_copies(k, slot):
        to = lax.rem(x + 1 + lax.div(k, kc), nx)
        at = pl.ds(pl.multiple_of(to * dx + lax.rem(k, kc) * cw, LANES), cw)
        return (
            pltpu.make_async_copy(wg_hbm.at[0, at, :], Vg.at[slot], vsem.at[slot, 0]),
            pltpu.make_async_copy(wu_hbm.at[0, at, :], Vu.at[slot], vsem.at[slot, 1]),
        )

    def core_copy(k):
        return remote(SC.at[k], RC.at[k], ccs.at[k], ccr.at[k], (g, 2 * z + 1 - c, x))

    def cx_copy(k):
        return remote(SX.at[k], RX.at[k], cxs.at[k], cxr.at[k], (g, e, lax.rem(x + 1 + k // kc, nx)))

    def cz_copy(j, d):
        to = lax.rem(z + d, nz)
        part = SZ.at[j, :, pl.ds(pl.multiple_of(to * hr, hr), hr), :]
        return remote(part, RZ.at[j, d - 1], czs.at[j, d], czr.at[j, d], (g, 2 * to + c, x))

    def piece(slot, h, cc):
        return acc[slot, pl.ds(pl.multiple_of(h * half + cc * mine, mine), mine), :]

    def stage_x(k):
        core_copy(k).wait_recv()
        for h in range(2):
            SX[k, h] = (piece(k % 2, h, c) + RC[k, h].astype(jnp.float32)).astype(jnp.bfloat16)
        cx_copy(k).start()

    def stage_z(k):
        j = k % kc
        core_copy(k).wait_recv()
        for d in range(nx - 1):
            cx_copy(d * kc + j).wait_recv()
        for h in range(2):
            total = piece(k % 2, h, c) + RC[k, h].astype(jnp.float32)
            for d in range(nx - 1):
                total = total + RX[d * kc + j, h].astype(jnp.float32)
            S2[j, h] = total
            SZ[j, h] = total.astype(jnp.bfloat16)
        for d in range(1, nz):
            cz_copy(j, d).start()

    def stage_out(j):
        for d in range(1, nz):
            cz_copy(j, d).wait_recv()
        for h in range(2):
            total = S2[j, h, pl.ds(pl.multiple_of(z * hr, hr), hr), :]
            for d in range(1, nz):
                total = total + RZ[j, d - 1, h].astype(jnp.float32)
            out_ref[h * hr:(h + 1) * hr, j * cw:(j + 1) * cw] = total.astype(jnp.bfloat16)

    def compute(h, slot, w, off):
        gate = jnp.dot(X[h, 0], Wg[slot, :, 0:w], preferred_element_type=jnp.float32)
        up = jnp.dot(X[h, 0], Wu[slot, :, 0:w], preferred_element_type=jnp.float32)
        back = contract_last(X[h, 1], Wd[slot, 0:w, :])
        sig = jax.nn.sigmoid(gate)
        act = gate * sig
        rp[h] += jnp.sum(act * up * back, axis=1, keepdims=True)
        scaled = wv[h][:, 0:1] * back
        here = pl.ds(pl.multiple_of(h * half, half), half)
        UG[here, pl.ds(off, w)] = (scaled * act).astype(jnp.bfloat16)
        GG[here, pl.ds(off, w)] = (scaled * up * sig * (1.0 + gate * (1.0 - sig))).astype(jnp.bfloat16)

    events = {}

    def plan(i, fn):
        events.setdefault(i, []).append(fn)

    for s in range(1, nz + 1):
        def event(s=s):
            if s < nz:
                step(1, s)
            xwait(1, s - 1)

        plan(min(s, nt - 1), event)
    plan(nt, lambda: cwait(1))

    def first_chunks():
        for k in range(min(2, steps)):
            for copy in chunk_copies(k, k):
                copy.start()

    plan(nt, first_chunks)

    def iteration(i, carry):
        h = lax.div(i, nt)
        t = lax.rem(i, nt)
        slot = lax.rem(i, 2) if nt > 1 else 0
        for at in sorted(events):
            @pl.when(i == at)
            def _():
                for fn in events[at]:
                    fn()

        if nt == 1:
            @pl.when(i == 0)
            def _():
                for copy in tile_copies(0, 0):
                    copy.wait()

            compute(h, 0, widths[0], 0)
            return carry

        following = lax.rem(t + 1, nt)
        other = 1 - slot

        @pl.when(jnp.logical_and(i + 1 < 2 * nt, following < nt - 1))
        def _():
            for copy in main_copies(following, other):
                copy.start()

        @pl.when(jnp.logical_and(i + 1 < 2 * nt, following == nt - 1))
        def _():
            for copy in tile_copies(nt - 1, other):
                copy.start()

        @pl.when(t < nt - 1)
        def _():
            for copy in main_copies(t, slot):
                copy.wait()
            compute(h, slot, widths[0], pl.multiple_of(t * widths[0], widths[0]))

        @pl.when(t == nt - 1)
        def _():
            for copy in tile_copies(nt - 1, slot):
                copy.wait()
            compute(h, slot, widths[nt - 1], sum(widths[:nt - 1]))

        return carry

    lax.fori_loop(0, 2 * nt, iteration, 0)

    for cc in range(2):
        for zz in range(nz):
            q = (cc * nz + zz) * hr
            row = jnp.zeros((1, LANES), jnp.float32)
            for h in range(2):
                row = row + jnp.sum(
                    jnp.where(hlane == hsub + h * hr, rp[h, q:q + hr, :], 0.0), axis=0, keepdims=True
                )
            RS[2 * zz + cc] = jnp.broadcast_to(row, (8, LANES))

    def pcopy(d):
        other = lax.rem(me + d, n)
        oe, ox = lax.div(other, nx), lax.rem(other, nx)
        return remote(RS.at[oe], RR.at[me], ps.at[other], pr.at[me], (g, oe, ox))

    def parrival(d):
        frm = lax.rem(me - d + n, n)
        fe, fx = lax.div(frm, nx), lax.rem(frm, nx)
        return remote(RS.at[fe], RR.at[frm], ps.at[frm], pr.at[frm], (g, fe, fx))

    lax.fori_loop(1, n, lambda d, carry: (pcopy(d).start(), carry)[1], 0)

    def after(k):
        if k // kc < nx - 1:
            stage_x(k)
        else:
            stage_z(k)

    def back_step(k, carry):
        slot = lax.rem(k, 2)
        for copy in chunk_copies(k, slot):
            copy.wait()
        acc[slot] = contract_last(GG[...], Vg[slot]) + contract_last(UG[...], Vu[slot])
        for h in range(2):
            SC[k, h] = piece(slot, h, 1 - c).astype(jnp.bfloat16)
        core_copy(k).start()

        @pl.when(k + 2 < steps)
        def _():
            for copy in chunk_copies(k + 2, slot):
                copy.start()

        for done in range(steps - 1):
            @pl.when(k == done + 1)
            def _():
                after(done)

        return carry

    lax.fori_loop(0, steps, back_step, 0)
    lax.fori_loop(1, n, lambda d, carry: (parrival(d).wait_recv(), carry)[1], 0)
    RR[me] = RS[e]
    after(steps - 1)
    grad = jnp.zeros(routes.shape, jnp.float32)
    for expert in range(ep):
        row = jnp.zeros((1, LANES), jnp.float32)
        for xx in range(nx):
            row = row + RR[expert * nx + xx][0:1, :]
        column = jnp.sum(jnp.where(lane == sub, row, 0.0), axis=1, keepdims=True)
        grad = grad + jnp.where(routes == expert, column, 0.0)
    rg_ref[...] = grad * (1.0 / math.sqrt(FF))

    for h in range(2):
        drain_gather(h)
    for k in range(steps):
        core_copy(k).wait_send()
    for k in range(steps - kc):
        cx_copy(k).wait_send()
    lax.fori_loop(1, ep, lambda d, carry: (bcopy(d).wait_send(), carry)[1], 0)
    lax.fori_loop(1, n, lambda d, carry: (pcopy(d).wait_send(), carry)[1], 0)
    for j in range(kc):
        stage_out(j)
        for d in range(1, nz):
            cz_copy(j, d).wait_send()


def shards(tokens, cotangent, routes, route_scale, gate_weight, up_weight, down_weight):
    ep, nx = lax.axis_size("ep"), lax.axis_size("fsdp")
    nz = ep // 2
    n = ep * nx
    block, dx = tokens.shape
    hr = block // 2
    depth, hidden = gate_weight.shape[1:]
    half = ep * hr
    mine = nz * hr
    if hidden % LANES == 0 and hidden > TILE:
        widths = [TILE] * (hidden // TILE) + ([hidden % TILE] if hidden % TILE else [])
    else:
        widths = [hidden]
    slots = min(2, len(widths))
    cw = TILE if dx % TILE == 0 else dx
    kc = dx // cw
    steps = kc * nx
    bf16, f32 = jnp.bfloat16, jnp.float32
    dma = pltpu.SemaphoreType.DMA
    vmem = pl.BlockSpec(memory_space=pltpu.VMEM)
    return pl.pallas_call(
        functools.partial(kernel, nz, nx, widths),
        out_shape=(
            jax.ShapeDtypeStruct((block, dx), bf16),
            jax.ShapeDtypeStruct(routes.shape, f32),
        ),
        in_specs=[vmem] * 4 + [pl.BlockSpec(memory_space=pl.ANY)] * 3,
        out_specs=(vmem, vmem),
        scratch_shapes=[
            pltpu.VMEM((2, 2, half, depth), bf16),
            pltpu.VMEM((slots, depth, widths[0]), bf16),
            pltpu.VMEM((slots, depth, widths[0]), bf16),
            pltpu.VMEM((slots, widths[0], depth), bf16),
            pltpu.VMEM((2, cw, hidden), bf16),
            pltpu.VMEM((2, cw, hidden), bf16),
            pltpu.VMEM((2 * half, hidden), bf16),
            pltpu.VMEM((2 * half, hidden), bf16),
            pltpu.VMEM((2, 2 * half, cw), f32),
            pltpu.VMEM((2, half, LANES), f32),
            pltpu.VMEM((2, half, LANES), f32),
            pltpu.VMEM((ep, 8, LANES), f32),
            pltpu.VMEM((ep, 8, LANES), f32),
            pltpu.VMEM((ep, 8, LANES), f32),
            pltpu.VMEM((n, 8, LANES), f32),
            pltpu.VMEM((steps, 2, mine, cw), bf16),
            pltpu.VMEM((steps, 2, mine, cw), bf16),
            pltpu.VMEM((steps - kc, 2, mine, cw), bf16),
            pltpu.VMEM((steps - kc, 2, mine, cw), bf16),
            pltpu.VMEM((kc, 2, mine, cw), f32),
            pltpu.VMEM((kc, 2, mine, cw), bf16),
            pltpu.VMEM((kc, nz - 1, 2, hr, cw), bf16),
            dma((slots, 3)),
            dma((2, 2)),
            dma((2, nz, 2)),
            dma((2, nz)),
            dma((2, nx, nz)),
            dma((2, nx, nz)),
            dma((2, nx, nz)),
            dma((2, nx, nz)),
            dma((ep,)),
            dma((ep,)),
            dma((n,)),
            dma((n,)),
            dma((steps,)),
            dma((steps,)),
            dma((steps,)),
            dma((steps,)),
            dma((kc, nz)),
            dma((kc, nz)),
        ],
        compiler_params=pltpu.CompilerParams(
            collective_id=0, has_side_effects=True, vmem_limit_bytes=62 * 1024 * 1024
        ),
        cost_estimate=pl.CostEstimate(
            flops=20 * half * depth * hidden, bytes_accessed=12 * depth * hidden, transcendentals=0
        ),
    )(tokens, cotangent, routes, route_scale, gate_weight, up_weight, down_weight)


def solution(mesh):
    in_specs = (
        P(("groups", "ep"), "fsdp"),
        P(("groups", "ep"), "fsdp"),
        P(("groups", "ep"), None),
        P(("groups", "ep"), None),
        P("ep", None, "fsdp"),
        P("ep", None, "fsdp"),
        P("ep", "fsdp", None),
    )
    out_specs = (P(("groups", "ep"), "fsdp"), P(("groups", "ep"), None))
    return jax.shard_map(shards, mesh=mesh, in_specs=in_specs, out_specs=out_specs, check_vma=False)
```

```python
import functools
import math

import jax
import jax.numpy as jnp
from jax import lax
from jax.experimental import pallas as pl
from jax.experimental.pallas import tpu as pltpu
from jax.sharding import PartitionSpec as P

FF = 5376
MESH = pl.DeviceIdType.MESH
LANES = 128
TILE = 512
CHUNK = 256


def contract_last(left, right):
    return lax.dot_general(
        left, right, (((1,), (1,)), ((), ())), preferred_element_type=jnp.float32
    )


def kernel(
    nz, nx, widths, tok_ref, cot_ref, routes_ref, scale_ref, wg_hbm, wu_hbm, wd_hbm,
    out_ref, rg_ref,
    X, Wg, Wu, Wd, Vg, Vu, GG, UG, acc, rp, wv, WS, WR, RS, RR, SC, RC, SX, RX, S2, SZ, RZ,
    wsem, vsem, zs, zr, xs, xr, cs, cr, bs, br, ps, pr, ccs, ccr, cxs, cxr, czs, czr,
):
    ep = 2 * nz
    n = ep * nx
    nt = len(widths)
    dx = tok_ref.shape[1]
    hr = tok_ref.shape[0] // 2
    mine = nz * hr
    half = 2 * mine
    cw = acc.shape[2]
    kc = dx // cw
    steps = kc * nx
    g = lax.axis_index("groups")
    e = lax.axis_index("ep")
    x = lax.axis_index("fsdp")
    z, c = lax.div(e, 2), lax.rem(e, 2)
    me = e * nx + x

    def rows(cc, zz, count=1):
        return pl.ds(pl.multiple_of((cc * nz + zz) * hr, hr), hr * count)

    def cols(xx):
        return pl.ds(pl.multiple_of(xx * dx, LANES), dx)

    def remote(src, dst, ss, rs, dev):
        return pltpu.make_async_remote_copy(
            src_ref=src, dst_ref=dst, send_sem=ss, recv_sem=rs,
            device_id=dev, device_id_type=MESH,
        )

    def tile_copies(t, slot):
        w, off = widths[t], sum(widths[:t])
        return (
            pltpu.make_async_copy(wg_hbm.at[0, :, pl.ds(off, w)], Wg.at[slot, :, pl.ds(0, w)], wsem.at[slot, 0]),
            pltpu.make_async_copy(wu_hbm.at[0, :, pl.ds(off, w)], Wu.at[slot, :, pl.ds(0, w)], wsem.at[slot, 1]),
            pltpu.make_async_copy(wd_hbm.at[0, pl.ds(off, w), :], Wd.at[slot, pl.ds(0, w), :], wsem.at[slot, 2]),
        )

    def main_copies(t, slot):
        w = widths[0]
        off = pl.multiple_of(t * w, w)
        return (
            pltpu.make_async_copy(wg_hbm.at[0, :, pl.ds(off, w)], Wg.at[slot, :, pl.ds(0, w)], wsem.at[slot, 0]),
            pltpu.make_async_copy(wu_hbm.at[0, :, pl.ds(off, w)], Wu.at[slot, :, pl.ds(0, w)], wsem.at[slot, 1]),
            pltpu.make_async_copy(wd_hbm.at[0, pl.ds(off, w), :], Wd.at[slot, pl.ds(0, w), :], wsem.at[slot, 2]),
        )

    barrier = pltpu.get_barrier_semaphore()

    def greet(d, carry):
        other = lax.rem(me + d, n)
        pl.semaphore_signal(
            barrier, inc=1, device_id=(g, lax.div(other, nx), lax.rem(other, nx)), device_id_type=MESH
        )
        return carry

    lax.fori_loop(1, n, greet, 0)

    for copy in tile_copies(0, 0):
        copy.start()

    for h in range(2):
        X[h, 0, rows(c, z), cols(x)] = tok_ref[h * hr:(h + 1) * hr, :]
        X[h, 1, rows(c, z), cols(x)] = cot_ref[h * hr:(h + 1) * hr, :]
    full = 2 * hr
    weights = scale_ref[...].astype(jnp.float32) / 4096.0
    routes = routes_ref[...]

    WS[...] = jnp.zeros_like(WS)
    for expert in range(ep):
        row = jnp.sum(jnp.where(routes == expert, weights, 0.0), axis=0, keepdims=True)
        WS[expert, :, 0:full] = jnp.broadcast_to(row, (8, full))

    rp[...] = jnp.zeros_like(rp)
    pl.semaphore_wait(barrier, n - 1)

    def zcopy(h, zb, way):
        part = X.at[h, :, rows(c, zb), cols(x)]
        to = z + 1 if way == 0 else z - 1
        return remote(part, part, zs.at[h, zb, way], zr.at[h, zb], (g, 2 * to + c, x))

    def xcopy(h, zb, d):
        part = X.at[h, :, rows(c, zb), cols(x)]
        return remote(part, part, xs.at[h, d, zb], xr.at[h, d, zb], (g, e, lax.rem(x + d, nx)))

    def xarrival(h, zb, d):
        part = X.at[h, :, rows(c, zb), cols(lax.rem(x - d + nx, nx))]
        return remote(part, part, xs.at[h, d, zb], xr.at[h, d, zb], (g, e, lax.rem(x + d, nx)))

    def ccopy(h, zb, xb):
        part = X.at[h, :, rows(c, zb), cols(xb)]
        return remote(part, part, cs.at[h, xb, zb], cr.at[h, xb, zb], (g, 2 * z + 1 - c, x))

    def carrival(h, zb, xb):
        part = X.at[h, :, rows(1 - c, zb), cols(xb)]
        return remote(part, part, cs.at[h, xb, zb], cr.at[h, xb, zb], (g, 2 * z + 1 - c, x))

    def spread(h, zb):
        for d in range(1, nx):
            xcopy(h, zb, d).start()
        ccopy(h, zb, x).start()

    def own(h):
        @pl.when(z < nz - 1)
        def _():
            zcopy(h, z, 0).start()

        @pl.when(z > 0)
        def _():
            zcopy(h, z, 1).start()

        spread(h, z)

    def step(h, s):
        @pl.when(z - s >= 0)
        def _():
            zcopy(h, z - s, 0).wait_recv()

            @pl.when(z < nz - 1)
            def _():
                zcopy(h, z - s, 0).start()

            spread(h, z - s)

        @pl.when(z + s < nz)
        def _():
            zcopy(h, z + s, 1).wait_recv()

            @pl.when(z > 0)
            def _():
                zcopy(h, z + s, 1).start()

            spread(h, z + s)

    def at_distance(s, fn):
        if s == 0:
            fn(z)
            return

        @pl.when(z - s >= 0)
        def _():
            fn(z - s)

        @pl.when(z + s < nz)
        def _():
            fn(z + s)

    def xwait(h, s):
        def one(zb):
            for d in range(1, nx):
                xarrival(h, zb, d).wait_recv()
                ccopy(h, zb, lax.rem(x - d + nx, nx)).start()

        at_distance(s, one)

    def cwait(h):
        for zb in range(nz):
            for xb in range(nx):
                carrival(h, zb, xb).wait_recv()

    def drain_gather(h):
        for zb in range(nz):
            @pl.when(jnp.logical_and(zb <= z, z < nz - 1))
            def _():
                zcopy(h, zb, 0).wait_send()

            @pl.when(jnp.logical_and(zb >= z, z > 0))
            def _():
                zcopy(h, zb, 1).wait_send()

            for d in range(1, nx):
                xcopy(h, zb, d).wait_send()
            for xb in range(nx):
                ccopy(h, zb, xb).wait_send()

    def bcopy(d):
        to = lax.rem(e + d, ep)
        return remote(WS.at[to], WR.at[e], bs.at[to], br.at[e], (g, to, x))

    def barrival(d):
        frm = lax.rem(e - d + ep, ep)
        return remote(WS.at[frm], WR.at[frm], bs.at[frm], br.at[frm], (g, frm, x))

    own(0)
    lax.fori_loop(1, ep, lambda d, carry: (bcopy(d).start(), carry)[1], 0)
    for s in range(1, nz):
        step(0, s)
        if s == nz - 1:
            own(1)
        xwait(0, s - 1)
    xwait(0, nz - 1)
    lax.fori_loop(1, ep, lambda d, carry: (barrival(d).wait_recv(), carry)[1], 0)
    WR[e] = WS[e]
    hlane = lax.broadcasted_iota(jnp.int32, (hr, LANES), 1)
    hsub = lax.broadcasted_iota(jnp.int32, (hr, LANES), 0)
    for cc in range(2):
        for zz in range(nz):
            row = WR[2 * zz + cc][0:1, :]
            for h in range(2):
                column = jnp.sum(jnp.where(hlane == hsub + h * hr, row, 0.0), axis=1, keepdims=True)
                q = (cc * nz + zz) * hr
                wv[h, q:q + hr, :] = jnp.broadcast_to(column, (hr, LANES))
    cwait(0)

    def chunk_copies(k, slot):
        to = lax.rem(x + 1 + lax.div(k, kc), nx)
        at = pl.ds(pl.multiple_of(to * dx + lax.rem(k, kc) * cw, LANES), cw)
        return (
            pltpu.make_async_copy(wg_hbm.at[0, at, :], Vg.at[slot], vsem.at[slot, 0]),
            pltpu.make_async_copy(wu_hbm.at[0, at, :], Vu.at[slot], vsem.at[slot, 1]),
        )

    def core_copy(k):
        return remote(SC.at[k], RC.at[k], ccs.at[k], ccr.at[k], (g, 2 * z + 1 - c, x))

    def cx_copy(k):
        return remote(SX.at[k], RX.at[k], cxs.at[k], cxr.at[k], (g, e, lax.rem(x + 1 + k // kc, nx)))

    def cz_copy(j, d):
        to = lax.rem(z + d, nz)
        part = SZ.at[j, :, pl.ds(pl.multiple_of(to * hr, hr), hr), :]
        return remote(part, RZ.at[j, d - 1], czs.at[j, d], czr.at[j, d], (g, 2 * to + c, x))

    def piece(slot, h, cc):
        return acc[slot, pl.ds(pl.multiple_of(h * half + cc * mine, mine), mine), :]

    def stage_x(k):
        core_copy(k).wait_recv()
        for h in range(2):
            SX[k, h] = (piece(k % 2, h, c) + RC[k, h].astype(jnp.float32)).astype(jnp.bfloat16)
        cx_copy(k).start()

    def stage_z(k):
        j = k % kc
        core_copy(k).wait_recv()
        for d in range(nx - 1):
            cx_copy(d * kc + j).wait_recv()
        for h in range(2):
            total = piece(k % 2, h, c) + RC[k, h].astype(jnp.float32)
            for d in range(nx - 1):
                total = total + RX[d * kc + j, h].astype(jnp.float32)
            S2[j, h] = total
            SZ[j, h] = total.astype(jnp.bfloat16)
        for d in range(1, nz):
            cz_copy(j, d).start()

    def stage_out(j):
        for d in range(1, nz):
            cz_copy(j, d).wait_recv()
        for h in range(2):
            total = S2[j, h, pl.ds(pl.multiple_of(z * hr, hr), hr), :]
            for d in range(1, nz):
                total = total + RZ[j, d - 1, h].astype(jnp.float32)
            out_ref[h * hr:(h + 1) * hr, j * cw:(j + 1) * cw] = total.astype(jnp.bfloat16)

    def compute(h, slot, w, off):
        gate = jnp.dot(X[h, 0], Wg[slot, :, 0:w], preferred_element_type=jnp.float32)
        up = jnp.dot(X[h, 0], Wu[slot, :, 0:w], preferred_element_type=jnp.float32)
        back = contract_last(X[h, 1], Wd[slot, 0:w, :])
        sig = jax.nn.sigmoid(gate)
        act = gate * sig
        rp[h] += jnp.sum(act * up * back, axis=1, keepdims=True)
        scaled = wv[h][:, 0:1] * back
        here = pl.ds(pl.multiple_of(h * half, half), half)
        UG[here, pl.ds(off, w)] = (scaled * act).astype(jnp.bfloat16)
        GG[here, pl.ds(off, w)] = (scaled * up * sig * (1.0 + gate * (1.0 - sig))).astype(jnp.bfloat16)

    events = {}

    def plan(i, fn):
        events.setdefault(i, []).append(fn)

    for s in range(1, nz):
        plan(min(s - 1, nt - 1), functools.partial(step, 1, s))
    for s in range(nz):
        plan(min(s + 1, nt - 1), functools.partial(xwait, 1, s))
    plan(nt, lambda: cwait(1))

    def first_chunks():
        for k in range(min(2, steps)):
            for copy in chunk_copies(k, k):
                copy.start()

    plan(nt, first_chunks)

    def iteration(i, carry):
        h = lax.div(i, nt)
        t = lax.rem(i, nt)
        slot = lax.rem(i, 2) if nt > 1 else 0
        for at in sorted(events):
            @pl.when(i == at)
            def _():
                for fn in events[at]:
                    fn()

        if nt == 1:
            @pl.when(i == 0)
            def _():
                for copy in tile_copies(0, 0):
                    copy.wait()

            compute(h, 0, widths[0], 0)
            return carry

        following = lax.rem(t + 1, nt)
        other = 1 - slot

        @pl.when(jnp.logical_and(i + 1 < 2 * nt, following < nt - 1))
        def _():
            for copy in main_copies(following, other):
                copy.start()

        @pl.when(jnp.logical_and(i + 1 < 2 * nt, following == nt - 1))
        def _():
            for copy in tile_copies(nt - 1, other):
                copy.start()

        @pl.when(t < nt - 1)
        def _():
            for copy in main_copies(t, slot):
                copy.wait()
            compute(h, slot, widths[0], pl.multiple_of(t * widths[0], widths[0]))

        @pl.when(t == nt - 1)
        def _():
            for copy in tile_copies(nt - 1, slot):
                copy.wait()
            compute(h, slot, widths[nt - 1], sum(widths[:nt - 1]))

        return carry

    lax.fori_loop(0, 2 * nt, iteration, 0)

    for cc in range(2):
        for zz in range(nz):
            q = (cc * nz + zz) * hr
            row = jnp.zeros((1, LANES), jnp.float32)
            for h in range(2):
                row = row + jnp.sum(
                    jnp.where(hlane == hsub + h * hr, rp[h, q:q + hr, :], 0.0), axis=0, keepdims=True
                )
            RS[2 * zz + cc] = jnp.broadcast_to(row, (8, LANES))

    def pcopy(d):
        other = lax.rem(me + d, n)
        oe, ox = lax.div(other, nx), lax.rem(other, nx)
        return remote(RS.at[oe], RR.at[me], ps.at[other], pr.at[me], (g, oe, ox))

    def parrival(d):
        frm = lax.rem(me - d + n, n)
        fe, fx = lax.div(frm, nx), lax.rem(frm, nx)
        return remote(RS.at[fe], RR.at[frm], ps.at[frm], pr.at[frm], (g, fe, fx))

    lax.fori_loop(1, n, lambda d, carry: (pcopy(d).start(), carry)[1], 0)

    def after(k):
        if k // kc < nx - 1:
            stage_x(k)
        else:
            stage_z(k)

    def back_step(k, carry):
        slot = lax.rem(k, 2)
        for copy in chunk_copies(k, slot):
            copy.wait()
        acc[slot] = contract_last(GG[...], Vg[slot]) + contract_last(UG[...], Vu[slot])
        for h in range(2):
            SC[k, h] = piece(slot, h, 1 - c).astype(jnp.bfloat16)
        core_copy(k).start()

        @pl.when(k + 2 < steps)
        def _():
            for copy in chunk_copies(k + 2, slot):
                copy.start()

        for done in range(steps - 1):
            @pl.when(k == done + 1)
            def _():
                after(done)

        return carry

    lax.fori_loop(0, steps, back_step, 0)
    lax.fori_loop(1, n, lambda d, carry: (parrival(d).wait_recv(), carry)[1], 0)
    RR[me] = RS[e]
    after(steps - 1)
    grad = jnp.zeros(routes.shape, jnp.float32)
    for expert in range(ep):
        row = jnp.zeros((1, LANES), jnp.float32)
        for xx in range(nx):
            row = row + RR[expert * nx + xx][0:1, :]
        grad = grad + jnp.where(routes == expert, row[:, 0:full], 0.0)
    rg_ref[...] = grad * (1.0 / math.sqrt(FF))

    for h in range(2):
        drain_gather(h)
    for k in range(steps):
        core_copy(k).wait_send()
    for k in range(steps - kc):
        cx_copy(k).wait_send()
    lax.fori_loop(1, ep, lambda d, carry: (bcopy(d).wait_send(), carry)[1], 0)
    lax.fori_loop(1, n, lambda d, carry: (pcopy(d).wait_send(), carry)[1], 0)
    for j in range(kc):
        stage_out(j)
        for d in range(1, nz):
            cz_copy(j, d).wait_send()


def shards(tokens, cotangent, routes, route_scale, gate_weight, up_weight, down_weight):
    ep, nx = lax.axis_size("ep"), lax.axis_size("fsdp")
    nz = ep // 2
    n = ep * nx
    block, dx = tokens.shape
    hr = block // 2
    depth, hidden = gate_weight.shape[1:]
    half = ep * hr
    mine = nz * hr
    if hidden % LANES == 0 and hidden > TILE:
        widths = [TILE] * (hidden // TILE) + ([hidden % TILE] if hidden % TILE else [])
    else:
        widths = [hidden]
    slots = min(2, len(widths))
    cw = CHUNK if dx % CHUNK == 0 else dx
    kc = dx // cw
    steps = kc * nx
    bf16, f32 = jnp.bfloat16, jnp.float32
    dma = pltpu.SemaphoreType.DMA
    vmem = pl.BlockSpec(memory_space=pltpu.VMEM)
    token_grad, route_grad = pl.pallas_call(
        functools.partial(kernel, nz, nx, widths),
        out_shape=(
            jax.ShapeDtypeStruct((block, dx), bf16),
            jax.ShapeDtypeStruct(routes.shape[::-1], f32),
        ),
        in_specs=[vmem] * 4 + [pl.BlockSpec(memory_space=pl.ANY)] * 3,
        out_specs=(vmem, vmem),
        scratch_shapes=[
            pltpu.VMEM((2, 2, half, depth), bf16),
            pltpu.VMEM((slots, depth, widths[0]), bf16),
            pltpu.VMEM((slots, depth, widths[0]), bf16),
            pltpu.VMEM((slots, widths[0], depth), bf16),
            pltpu.VMEM((2, cw, hidden), bf16),
            pltpu.VMEM((2, cw, hidden), bf16),
            pltpu.VMEM((2 * half, hidden), bf16),
            pltpu.VMEM((2 * half, hidden), bf16),
            pltpu.VMEM((2, 2 * half, cw), f32),
            pltpu.VMEM((2, half, LANES), f32),
            pltpu.VMEM((2, half, LANES), f32),
            pltpu.VMEM((ep, 8, LANES), f32),
            pltpu.VMEM((ep, 8, LANES), f32),
            pltpu.VMEM((ep, 8, LANES), f32),
            pltpu.VMEM((n, 8, LANES), f32),
            pltpu.VMEM((steps, 2, mine, cw), bf16),
            pltpu.VMEM((steps, 2, mine, cw), bf16),
            pltpu.VMEM((steps - kc, 2, mine, cw), bf16),
            pltpu.VMEM((steps - kc, 2, mine, cw), bf16),
            pltpu.VMEM((kc, 2, mine, cw), f32),
            pltpu.VMEM((kc, 2, mine, cw), bf16),
            pltpu.VMEM((kc, nz - 1, 2, hr, cw), bf16),
            dma((slots, 3)),
            dma((2, 2)),
            dma((2, nz, 2)),
            dma((2, nz)),
            dma((2, nx, nz)),
            dma((2, nx, nz)),
            dma((2, nx, nz)),
            dma((2, nx, nz)),
            dma((ep,)),
            dma((ep,)),
            dma((n,)),
            dma((n,)),
            dma((steps,)),
            dma((steps,)),
            dma((steps,)),
            dma((steps,)),
            dma((kc, nz)),
            dma((kc, nz)),
        ],
        compiler_params=pltpu.CompilerParams(
            collective_id=0, has_side_effects=True, vmem_limit_bytes=62 * 1024 * 1024
        ),
        cost_estimate=pl.CostEstimate(
            flops=20 * half * depth * hidden, bytes_accessed=12 * depth * hidden, transcendentals=0
        ),
    )(tokens, cotangent, routes.T, route_scale.T, gate_weight, up_weight, down_weight)
    return token_grad, route_grad.T


def solution(mesh):
    in_specs = (
        P(("groups", "ep"), "fsdp"),
        P(("groups", "ep"), "fsdp"),
        P(("groups", "ep"), None),
        P(("groups", "ep"), None),
        P("ep", None, "fsdp"),
        P("ep", None, "fsdp"),
        P("ep", "fsdp", None),
    )
    out_specs = (P(("groups", "ep"), "fsdp"), P(("groups", "ep"), None))
    return jax.shard_map(shards, mesh=mesh, in_specs=in_specs, out_specs=out_specs, check_vma=False)
```
